32 devices in a mesh: dp: 4 (over y, x), tensor: 8 (over z, core).
Axes of the slice: x: 2, y: 2, z: 4, core: 2. Of those that a mesh axis runs over, the one named last changes fastest.
Arguments:
- activations: bfloat16 [3, 192, 8192], P(None, 'dp'), may hold values from -6 to 6
- hidden_grad: bfloat16 [3, 192, 11520], P(None, 'dp', 'tensor'), may hold values from -6 to 6
- weight: bfloat16 [11520, 8192], P('tensor'), may hold values from -0.078125 to 0.078125
- master: float32 [11520, 8192], P(('tensor', 'dp')), may hold values from -6 to 6
- first_moment: float32 [11520, 8192], P(('tensor', 'dp')), may hold values from -0.05 to 0.05
- second_moment: float32 [11520, 8192], P(('tensor', 'dp')), may hold values from 0.00052083336 to 0.0052083335
- ema_state: float32 [11520, 8192], P(('tensor', 'dp')), may hold values from -6 to 6
Outputs:
- d_inputs: bfloat16 [3, 192, 8192], P(None, 'dp', 'tensor')
- master_out: float32 [11520, 8192], P(('tensor', 'dp'))
- new_first: float32 [11520, 8192], P(('tensor', 'dp'))
- new_second: float32 [11520, 8192], P(('tensor', 'dp'))
- ema_copy: bfloat16 [11520, 8192], P('tensor')
The draws below stay inside these ranges and needn't reach their ends.
All inputs are finite; a program needn't handle non-finite values.
Results may differ from the reference program's by a relative error of at most 0.0065.
Values may be sent and summed in bfloat16 or wider, within the bound.
No kernel may reach another device: no remote copies, remote signals or barrier semaphores. Data moves between devices by JAX's collectives and lax.ppermute only.
A program may use at most 256 MiB of HBM per device.

```python
import math
import jax
import jax.numpy as jnp
from jax import lax

D = 8192
FF = 11520
MB = 3
TOK_DEV = 48
TOKENS = 192
N_DP = 4


def strengthened(array, stream_key, source, target, shards_of, factor):
    owner, partner = [(jnp.arange(array.shape[dim]) // (array.shape[dim] // shards_of)).reshape([-1 if axis == dim else 1 for axis in range(array.ndim)]) for dim in (source, target)]
    chosen = jax.random.permutation(stream_key, shards_of)[partner]
    strong = (owner == chosen) | (owner == (partner + shards_of // 2) % shards_of)
    return jnp.where(strong, factor * array, array)


def block_scale(rng, shape, split, least, top_value):
    def one(dim, shards_of):
        draws = jax.random.uniform(jax.random.fold_in(jax.random.fold_in(rng, 6), dim), (shards_of,), jnp.float32, least / len(split), top_value / len(split))
        return jnp.repeat(jnp.exp(draws), shape[dim] // shards_of).reshape((-1,) + (1,) * (len(shape) - dim - 1))

    factor_of = one(*split[0])
    for cut in split[1:]:
        factor_of = factor_of * one(*cut)
    return factor_of


def scatter_about(rng, dims, scale, limit, pieces=(), dtype=jnp.bfloat16):
    entries = jax.random.normal(rng, dims, jnp.float32) * scale
    if len(pieces) > 0:
        entries = block_scale(rng, dims, pieces, -0.22, 0.18) * entries
    return jnp.clip(entries, min=-limit, max=limit).astype(dtype)


def heavy_noise(own_key, shape, spread, reach, split, heavy, held_as=jnp.bfloat16):
    drawn = spread * jax.random.normal(own_key, shape, jnp.float32)
    if split:
        drawn = drawn * block_scale(own_key, shape, split, -0.22, 0.18)
    return jnp.clip(strengthened(drawn, jax.random.fold_in(own_key, 3), *heavy), -reach, reach).astype(held_as)


def setup_inputs(seed: int = 0) -> dict:
    streams_of = jax.random.split(jax.random.key(seed), 8)
    return {
        "activations": scatter_about(streams_of[0], (MB, TOKENS, D), 1.0, 6.0, ((1, 4),)),
        "hidden_grad": scatter_about(streams_of[1], (MB, TOKENS, FF), 1.0, 6.0, ((1, 4), (2, 8))),
        "weight": heavy_noise(streams_of[2], (FF, D), FF ** -0.5, 0.078125, ((0, 8),), (0, 1, 8, 2.0)),
        "master": scatter_about(streams_of[3], (FF, D), 1.0, 6.0, ((0, 32),), jnp.float32),
        "first_moment": scatter_about(streams_of[4], (FF, D), (0.2 / (MB * TOKENS) ** 0.5), 0.05, ((0, 32),), jnp.float32),
        "second_moment": jnp.clip(jnp.exp(math.log(0.0052083335) - 2.3025851 * jax.random.uniform(streams_of[5], (FF, D), jnp.float32) ** block_scale(streams_of[5], (FF, D), ((0, 32),), -0.2, 0.2)), 0.00052083336, 0.0052083335),
        "ema_state": scatter_about(streams_of[6], (FF, D), 1.0, 6.0, ((0, 32),), jnp.float32),
    }


beta_one = 0.9
beta_two = 0.95
adam_step = 20.0
learn_rate = 0.1
decay_rate = 0.1
epsilon = 1e-08
ema_keep = 0.99

def reference(activations, hidden_grad, weight, master, first_moment, second_moment, ema_state):
    inverse = 1.0 / (MB * TOKENS)
    outputs = []
    for batch_id in range(MB):
        product = jnp.dot(hidden_grad[batch_id], weight, preferred_element_type=jnp.float32)
        outputs.append(product.astype(jnp.bfloat16))
    d_inputs = jnp.stack(outputs)
    gradient = jnp.zeros((FF, D), jnp.float32)
    for block_id in range(N_DP):
        acts_block = activations[:, block_id * TOK_DEV:(block_id + 1) * TOK_DEV, :].reshape(MB * TOK_DEV, D)
        grad_block = hidden_grad[:, block_id * TOK_DEV:(block_id + 1) * TOK_DEV, :].reshape(MB * TOK_DEV, FF)
        partial_value = jnp.dot(grad_block.T, acts_block, preferred_element_type=jnp.float32) * inverse
        rounded = lax.optimization_barrier(partial_value.astype(jnp.bfloat16))
        gradient = gradient + rounded.astype(jnp.float32)
    new_first = beta_one * first_moment + (1.0 - beta_one) * gradient
    new_second = beta_two * second_moment + (1.0 - beta_two) * gradient * gradient
    first_fix = 1.0 - beta_one ** adam_step
    second_fix = 1.0 - beta_two ** adam_step
    update = new_first / first_fix / (jnp.sqrt(new_second / second_fix) + epsilon) + decay_rate * master
    master_out = master - learn_rate * update
    ema_next = ema_keep * ema_state + (1.0 - ema_keep) * master_out
    return (d_inputs, master_out, new_first, new_second, ema_next.astype(jnp.bfloat16))
```

```python
import functools

import jax
import jax.numpy as jnp
from jax import lax
from jax.experimental import pallas as pl
from jax.experimental.pallas import tpu as pltpu
from jax.sharding import PartitionSpec as P

beta_one = 0.9
beta_two = 0.95
adam_step = 20.0
learn_rate = 0.1
decay_rate = 0.1
epsilon = 1e-08
ema_keep = 0.99
first_fix = 1.0 - beta_one**adam_step
second_fix = 1.0 - beta_two**adam_step

TILE = 256
FIRST_CUTS = (4, 4, 2)
LAST_CUTS = (2, 4, 4)
LAG = 3
PRODUCT_AFTER = 2
VMEM_LIMIT = 58 * 1024 * 1024
ANY = pl.BlockSpec(memory_space=pl.ANY)


def adam(gradient, master, first_moment, second_moment, ema_state):
    new_first = beta_one * first_moment + (1.0 - beta_one) * gradient
    new_second = beta_two * second_moment + (1.0 - beta_two) * gradient * gradient
    update = (
        new_first / first_fix / (jnp.sqrt(new_second / second_fix) + epsilon) + decay_rate * master
    )
    master_out = master - learn_rate * update
    ema_next = ema_keep * ema_state + (1.0 - ema_keep) * master_out
    return master_out, new_first, new_second, ema_next


def step_kernel(inverse, n_unread, place, grads, acts, master, first, second, ema, *rest):
    piece, master_out, first_out, second_out = rest[n_unread:]
    total = None
    for i in range(grads.shape[0]):
        term = jnp.dot(grads[i], acts[i], preferred_element_type=jnp.float32)
        total = term if total is None else total + term
    outs = adam(total * inverse, master[...], first[...], second[...], ema[...])
    master_out[...] = outs[0]
    first_out[...] = outs[1]
    second_out[...] = outs[2]
    piece[...] = outs[3].astype(piece.dtype)


def optimizer_step(inverse, place, offset, width, grads, acts, states, olds, after):
    rows, model_width = states[0].shape
    parts, _, tokens = grads.shape
    state_spec = pl.BlockSpec((rows, TILE), lambda j, place: (0, place[0] + j))
    first_tile = offset // TILE
    shape = jax.ShapeDtypeStruct((rows, model_width), jnp.float32)
    n_old = len(olds)
    return pl.pallas_call(
        functools.partial(step_kernel, inverse, n_old + len(after)),
        out_shape=(jax.ShapeDtypeStruct((rows, width), jnp.bfloat16), shape, shape, shape),
        grid_spec=pltpu.PrefetchScalarGridSpec(
            num_scalar_prefetch=1,
            grid=(width // TILE,),
            in_specs=[
                pl.BlockSpec((parts, rows, tokens), lambda j, place: (0, 0, 0)),
                pl.BlockSpec((parts, tokens, TILE), lambda j, place: (0, 0, first_tile + j)),
            ]
            + [state_spec] * 4
            + [ANY] * (n_old + len(after)),
            out_specs=[pl.BlockSpec((rows, TILE), lambda j, place: (0, j))] + [state_spec] * 3,
        ),
        input_output_aliases={7 + i: 1 + i for i in range(n_old)},
        compiler_params=pltpu.CompilerParams(vmem_limit_bytes=VMEM_LIMIT),
        cost_estimate=pl.CostEstimate(
            flops=2 * parts * rows * tokens * width,
            bytes_accessed=rows * width * 30 + parts * tokens * (width + rows) * 2,
            transcendentals=rows * width,
        ),
        name="optimizer_step",
    )(place, grads, acts, *states, *olds, *after)


def place_kernel(n_pieces, n_old, width, where, *rest):
    pieces = rest[:n_pieces]
    out, token, held, arrived, left = rest[n_pieces + n_old :]
    column = pl.multiple_of(where[n_pieces] * TILE, TILE)
    loads = [
        pltpu.make_async_copy(piece, held.at[i], arrived.at[i]) for i, piece in enumerate(pieces)
    ]
    stores = [
        pltpu.make_async_copy(held.at[i], out.at[where[i], :, pl.ds(column, width)], left.at[i])
        for i in range(n_pieces)
    ]
    for load in loads:
        load.start()
    token[...] = jnp.zeros_like(token)
    for load, store in zip(loads, stores):
        load.wait()
        store.start()
    for store in stores:
        store.wait()


def place_pieces(where, pieces, old, shape):
    rows, width = pieces[0].shape
    n_pieces = len(pieces)
    olds = () if old is None else (old,)
    n_old = len(olds)
    return pl.pallas_call(
        functools.partial(place_kernel, n_pieces, n_old, width),
        out_shape=(
            jax.ShapeDtypeStruct(shape, jnp.bfloat16),
            jax.ShapeDtypeStruct((8, 128), jnp.float32),
        ),
        grid_spec=pltpu.PrefetchScalarGridSpec(
            num_scalar_prefetch=1,
            grid=(),
            in_specs=[ANY] * (n_pieces + n_old),
            out_specs=(ANY, pl.BlockSpec(memory_space=pltpu.VMEM)),
            scratch_shapes=[
                pltpu.VMEM((n_pieces, rows, width), jnp.bfloat16),
                pltpu.SemaphoreType.DMA((n_pieces,)),
                pltpu.SemaphoreType.DMA((n_pieces,)),
            ],
        ),
        input_output_aliases={1 + n_pieces: 0} if n_old else {},
        compiler_params=pltpu.CompilerParams(vmem_limit_bytes=VMEM_LIMIT),
        cost_estimate=pl.CostEstimate(
            flops=0, bytes_accessed=n_pieces * rows * width * 4, transcendentals=0
        ),
        name="place_pieces",
    )(where, *pieces, *olds)


def product_kernel(half, order, grads, weight, after, keep, send):
    step = pl.program_id(0)
    product = jnp.dot(grads[...], weight[...], preferred_element_type=jnp.float32)

    @pl.when(step < half)
    def _():
        send[0] = product.astype(send.dtype)

    @pl.when(step >= half)
    def _():
        keep[0] = product


def input_product(order, grads, weight, after):
    tokens, units = grads.shape
    slices = order.shape[0]
    half = slices // 2
    width = weight.shape[1] // slices
    return pl.pallas_call(
        functools.partial(product_kernel, half),
        out_shape=(
            jax.ShapeDtypeStruct((half, tokens, width), jnp.float32),
            jax.ShapeDtypeStruct((half, tokens, width), jnp.bfloat16),
        ),
        grid_spec=pltpu.PrefetchScalarGridSpec(
            num_scalar_prefetch=1,
            grid=(slices,),
            in_specs=[
                pl.BlockSpec((tokens, units), lambda j, order: (0, 0)),
                pl.BlockSpec((units, width), lambda j, order: (0, order[j])),
                ANY,
            ],
            out_specs=[
                pl.BlockSpec((1, tokens, width), lambda j, order: (jnp.maximum(j - half, 0), 0, 0)),
                pl.BlockSpec((1, tokens, width), lambda j, order: (jnp.minimum(j, half - 1), 0, 0)),
            ],
        ),
        compiler_params=pltpu.CompilerParams(vmem_limit_bytes=VMEM_LIMIT),
        cost_estimate=pl.CostEstimate(
            flops=2 * tokens * units * width * slices,
            bytes_accessed=units * width * slices * 2 + tokens * width * slices * 3,
            transcendentals=0,
        ),
        name="input_product",
    )(order, grads, weight, after)


def square_body(activations, hidden_grad, weight, master, first_moment, second_moment, ema_state):
    batches, tok_rows, model_width = activations.shape
    shard_units = master.shape[0]
    n_dp = lax.axis_size("dp")
    n_tensor = lax.axis_size("tensor")
    n_pairs = n_tensor // 2
    tokens = batches * tok_rows
    inverse = 1.0 / (tokens * n_dp)
    width = model_width // n_tensor
    dp = lax.axis_index("dp")
    tensor = lax.axis_index("tensor")
    pair, core = tensor // 2, tensor % 2

    def swap(array, mask):
        return lax.ppermute(array, "dp", [(i, i ^ mask) for i in range(n_dp)])

    def swap_core(array):
        return lax.ppermute(array, "tensor", [(i, i ^ 1) for i in range(n_tensor)])

    def shift_pair(array, steps):
        moves = [(i, (i + 2 * steps) % n_tensor) for i in range(n_tensor)]
        return lax.ppermute(array, "tensor", moves)

    acts_two = activations.reshape(tokens, model_width)
    grads_two = hidden_grad.reshape(tokens, -1)
    grads_turned = grads_two.T.reshape(n_dp, shard_units, tokens)
    own_acts = lax.dynamic_slice_in_dim(acts_two, tensor * width, width, 1)

    def units_of(mask):
        return lax.dynamic_index_in_dim(grads_turned, dp ^ mask, 0, keepdims=False)

    grads = jnp.stack([units_of(0)] + [swap(units_of(m), m) for m in range(1, n_dp)])
    acts = jnp.stack([own_acts] + [swap(own_acts, m) for m in range(1, n_dp)])

    pairs = (pair + jnp.arange(n_pairs)) % n_pairs
    order = jnp.concatenate([pairs * 2 + (core ^ 1), pairs * 2 + core]).astype(jnp.int32)
    states = (master, first_moment, second_moment, ema_state)
    shape = (n_dp, shard_units, model_width)
    olds, out, tokens_placed = (), None, []
    count = 0
    for step in range(n_pairs):
        if step > 0:
            acts = shift_pair(acts, 1)
        for side in range(2):
            block = acts if side == 0 else swap_core(acts)
            feature = ((pair - step) % n_pairs) * 2 + (core ^ side)
            chunk = 2 * step + side
            parts = FIRST_CUTS if chunk == 0 else LAST_CUTS if chunk == n_tensor - 1 else (1,)
            offset = 0
            for part in parts:
                cut_width = width // part
                tile = (feature * width + offset) // TILE
                place = jnp.stack([tile]).astype(jnp.int32)
                after = tokens_placed[count - LAG : count - LAG + 1] if count >= LAG else []
                piece, *olds = optimizer_step(
                    inverse, place, offset, cut_width, grads, block, states, tuple(olds), after
                )
                by_x, by_y = swap(piece, 1), swap(piece, 2)
                by_both = swap(by_x, 2) if count % 2 else swap(by_y, 1)
                where = jnp.stack([dp, dp ^ 1, dp ^ 2, dp ^ 3, tile]).astype(jnp.int32)
                out, token = place_pieces(where, (piece, by_x, by_y, by_both), out, shape)
                tokens_placed.append(token)
                if count == PRODUCT_AFTER:
                    keep, send = input_product(order, grads_two, weight, piece)
                offset += cut_width
                count += 1
    ema_copy = out.reshape(n_dp * shard_units, model_width)

    both = keep + swap_core(send).astype(jnp.float32)
    total = both[0]
    for step in range(1, n_pairs):
        total = total + shift_pair(both[step].astype(jnp.bfloat16), step).astype(jnp.float32)
    d_inputs = total.astype(jnp.bfloat16).reshape(batches, tok_rows, width)
    return (d_inputs, *olds, ema_copy)


def general_body(activations, hidden_grad, weight, master, first_moment, second_moment, ema_state):
    batches, tok_rows, model_width = activations.shape
    shard_units = master.shape[0]
    inverse = 1.0 / (batches * tok_rows * lax.axis_size("dp"))
    pieces = []
    for batch_id in range(batches):
        product = jnp.dot(hidden_grad[batch_id], weight, preferred_element_type=jnp.float32)
        pieces.append(
            lax.psum_scatter(product, "tensor", scatter_dimension=1, tiled=True).astype(
                jnp.bfloat16
            )
        )
    d_inputs = jnp.stack(pieces)
    col_start = lax.axis_index("dp") * shard_units
    acts_piece = lax.all_gather(activations, "dp", axis=1, tiled=True)
    grad_piece = lax.all_gather(hidden_grad, "dp", axis=1, tiled=True)
    shards = acts_piece.shape[1] // tok_rows
    columns = lax.dynamic_slice_in_dim(grad_piece, col_start, shard_units, 2)
    acts_blocks = acts_piece.reshape(batches, shards, tok_rows, model_width)
    grad_blocks = columns.reshape(batches, shards, tok_rows, shard_units)
    per_shard = (
        jnp.einsum("bstf,bstd->sfd", grad_blocks, acts_blocks, preferred_element_type=jnp.float32)
        * inverse
    )
    rounded = lax.optimization_barrier(per_shard.astype(jnp.bfloat16))
    gradient = jnp.sum(rounded.astype(jnp.float32), axis=0)
    master_out, new_first, new_second, ema_next = adam(
        gradient, master, first_moment, second_moment, ema_state
    )
    ema_copy = lax.all_gather(ema_next.astype(jnp.bfloat16), "dp", axis=0, tiled=True)
    return (d_inputs, master_out, new_first, new_second, ema_copy)


def body(*arrays):
    activations, _, _, master = arrays[:4]
    n_tensor = lax.axis_size("tensor")
    square = (
        lax.axis_size("dp") == 4
        and n_tensor % 2 == 0
        and master.shape[0] % 8 == 0
        and activations.shape[2] % (n_tensor * 4 * TILE) == 0
    )
    return square_body(*arrays) if square else general_body(*arrays)


def solution(mesh):
    return jax.shard_map(
        body,
        mesh=mesh,
        in_specs=(
            P(None, "dp", None),
            P(None, "dp", "tensor"),
            P("tensor", None),
            P(("tensor", "dp"), None),
            P(("tensor", "dp"), None),
            P(("tensor", "dp"), None),
            P(("tensor", "dp"), None),
        ),
        out_specs=(
            P(None, "dp", "tensor"),
            P(("tensor", "dp"), None),
            P(("tensor", "dp"), None),
            P(("tensor", "dp"), None),
            P("tensor", None),
        ),
        check_vma=False,
    )
```

```python
import functools

import jax
import jax.numpy as jnp
from jax import lax
from jax.experimental import pallas as pl
from jax.experimental.pallas import tpu as pltpu
from jax.sharding import PartitionSpec as P

beta_one = 0.9
beta_two = 0.95
adam_step = 20.0
learn_rate = 0.1
decay_rate = 0.1
epsilon = 1e-08
ema_keep = 0.99
first_fix = 1.0 - beta_one**adam_step
second_fix = 1.0 - beta_two**adam_step

LEAD = 256
LAG = 3
PRODUCT_FIRST = 6
PRODUCT_AT = 3
FIRST_CUTS = (2, 2)
LAST_CUTS = (4,)
UNPACK_AT = 0
GATE = 2
FORWARD_BY_X = (1,0,1,0,1,0,1,0,1,0,1,0)
LAST_MORE = 0
TAIL_SPLIT = 2
STEP_COST = 8000000
PLACE_COST = 850
PRODUCT_COST = 6000000
VMEM_LIMIT = 58 * 1024 * 1024
ANY = pl.BlockSpec(memory_space=pl.ANY)
PARAMS = pltpu.CompilerParams(vmem_limit_bytes=VMEM_LIMIT)


def adam(gradient, master, first_moment, second_moment, ema_state):
    new_first = beta_one * first_moment + (1.0 - beta_one) * gradient
    new_second = beta_two * second_moment + (1.0 - beta_two) * gradient * gradient
    update = (
        new_first / first_fix / (jnp.sqrt(new_second / second_fix) + epsilon) + decay_rate * master
    )
    master_out = master - learn_rate * update
    ema_next = ema_keep * ema_state + (1.0 - ema_keep) * master_out
    return master_out, new_first, new_second, ema_next


def feature_of(ids, n_tensor, step, side):
    n_pairs = n_tensor // 2
    pair = lax.rem(lax.div(ids[1], 2) + (n_pairs - step), n_pairs)
    core = lax.rem(ids[1], 2)
    return 2 * pair + (1 - core if side else core)


def peer_of(dp, mask):
    high, low = lax.div(dp, 2), lax.rem(dp, 2)
    return 2 * (1 - high if mask & 2 else high) + (1 - low if mask & 1 else low)


def pack_kernel(units, width, ids, acts, grads, *messages):
    for mask, message in enumerate(messages):
        message[:, :width] = acts[...]
        for owner in range(len(messages)):

            @pl.when(peer_of(ids[0], mask) == owner)
            def _(owner=owner, message=message):
                message[:, width : width + units] = grads[:, owner * units : (owner + 1) * units]


def pack_messages(ids, acts, grads, n_dp, width):
    tokens, all_units = grads.shape
    units = all_units // n_dp
    message = jax.ShapeDtypeStruct((tokens, width + pl.cdiv(units, 128) * 128), acts.dtype)
    return pl.pallas_call(
        functools.partial(pack_kernel, units, width),
        out_shape=(message,) * n_dp,
        grid_spec=pltpu.PrefetchScalarGridSpec(
            num_scalar_prefetch=1,
            grid=(1,),
            in_specs=[
                pl.BlockSpec((tokens, width), lambda j, ids: (0, ids[1])),
                pl.BlockSpec((tokens, all_units), lambda j, ids: (0, 0)),
            ],
            out_specs=[pl.BlockSpec(message.shape, lambda j, ids: (0, 0))] * n_dp,
        ),
        compiler_params=PARAMS,
        cost_estimate=pl.CostEstimate(
            flops=0, bytes_accessed=tokens * all_units * 8, transcendentals=0
        ),
        name="pack_messages",
    )(ids, acts, grads)


def column_of(ids, where, slice_width):
    n_tensor, step, side, offset = where
    return pl.multiple_of(feature_of(ids, n_tensor, step, side) * slice_width + offset, LEAD)


def place_scratch(groups):
    scratch = []
    for _, masks, pieces in groups:
        scratch.append(pltpu.VMEM((len(masks),) + pieces[0].shape, pieces[0].dtype))
        scratch.append(pltpu.SemaphoreType.DMA((len(masks),)))
        scratch.append(pltpu.SemaphoreType.DMA((len(masks),)))
    return scratch


def placements(ids, slice_width, layout, pieces, out, scratch):
    loads, stores = [], []
    for i, (where, masks) in enumerate(layout):
        held, arrived, left = scratch[3 * i : 3 * i + 3]
        column = column_of(ids, where, slice_width)
        for j, mask in enumerate(masks):
            piece = pieces[len(loads)]
            goal = out.at[peer_of(ids[0], mask), :, pl.ds(column, piece.shape[1])]
            loads.append(pltpu.make_async_copy(piece, held.at[j], arrived.at[j]))
            stores.append(pltpu.make_async_copy(held.at[j], goal, left.at[j]))
    return loads, stores


def forward_copies(loads, stores):
    for load, store in zip(loads, stores):
        load.wait()
        store.start()


def step_kernel(
    inverse, units, slice_width, offset, unpack, n_acts, n_unread, layout, n_steps, ids, *refs
):
    acts = refs[:n_acts]
    refs = refs[n_acts:]
    if units is None:
        gradient = lambda: jnp.dot(refs[0][...], acts[0][...], preferred_element_type=jnp.float32)
        refs_states = refs[1:5]
        rest = refs[5:]
    else:

        def gradient():
            total = None
            for message in acts:
                term = lax.dot_general(
                    message[:, slice_width : slice_width + units],
                    message[:, offset : offset + tile],
                    (((0,), (0,)), ((), ())),
                    preferred_element_type=jnp.float32,
                )
                total = term if total is None else total + term
            return total

        refs_states = refs[:4]
        rest = refs[4:]
    master, first, second, ema = refs_states
    n_pieces = sum(len(masks) for _, masks in layout)
    pieces = rest[:n_pieces]
    rest = rest[n_pieces + n_unread :]
    piece, master_out, first_out, second_out = rest[:4]
    tile = piece.shape[1]
    step = pl.program_id(0)
    if n_pieces:
        loads, stores = placements(ids, slice_width, layout, pieces, rest[4], rest[5:])

        @pl.when(step == 0)
        def _():
            for load in loads:
                load.start()

        if n_steps > 1:

            @pl.when(step == n_steps - 1)
            def _():
                forward_copies(loads, stores)

    outs = adam(gradient() * inverse, master[...], first[...], second[...], ema[...])
    master_out[...] = outs[0]
    first_out[...] = outs[1]
    second_out[...] = outs[2]
    piece[...] = outs[3].astype(piece.dtype)
    if unpack:
        all_acts, all_grads = rest[-2:]
        tokens = acts[0].shape[0]
        for i, message in enumerate(acts):
            rows = slice(i * tokens, (i + 1) * tokens)
            all_acts[rows, :] = message[:, :slice_width]
            all_grads[:, rows] = message[:, slice_width : slice_width + units].T
    if n_pieces:

        @pl.when(step == n_steps - 1)
        def _():
            if n_steps == 1:
                forward_copies(loads, stores)
            for store in stores:
                store.wait()


def optimizer_step(
    inverse, units, unpack, ids, where, width, acts, grads, states, olds, unread, groups, whole_shape, out
):
    rows, model_width = states[0].shape
    n_tensor, step, side, offset = where
    slice_width = model_width // n_tensor
    tile = 2 * LEAD if width % (2 * LEAD) == 0 and offset % (2 * LEAD) == 0 else LEAD
    n_steps = width // tile

    def state_at(j, ids):
        return 0, feature_of(ids, n_tensor, step, side) * (slice_width // tile) + offset // tile + j

    def whole(array):
        return pl.BlockSpec(array.shape, lambda j, ids: (0,) * array.ndim)

    state_spec = pl.BlockSpec((rows, tile), state_at)
    if units is None:
        first_tile = offset // tile
        in_specs = [
            pl.BlockSpec((acts[0].shape[0], tile), lambda j, ids: (0, first_tile + j)),
            whole(grads),
        ]
        operands = [acts[0], grads]
    else:
        in_specs = [whole(message) for message in acts]
        operands = list(acts)
    n_acts = len(acts)
    operands += list(states)
    in_specs += [state_spec] * 4
    out_shapes = [jax.ShapeDtypeStruct((rows, width), jnp.bfloat16)]
    out_shapes += [jax.ShapeDtypeStruct((rows, model_width), jnp.float32)] * 3
    out_specs = [pl.BlockSpec((rows, tile), lambda j, ids: (0, j))] + [state_spec] * 3
    pieces = [piece for group in groups for piece in group[2]]
    if groups:
        out_shapes.append(jax.ShapeDtypeStruct(whole_shape, jnp.bfloat16))
        out_specs.append(ANY)
    if unpack:
        tokens = n_acts * acts[0].shape[0]
        for shape in ((tokens, slice_width), (units, tokens)):
            out_shapes.append(jax.ShapeDtypeStruct(shape, jnp.bfloat16))
            out_specs.append(pl.BlockSpec(shape, lambda j, ids: (0, 0)))
    operands += pieces
    aliases = {}
    extra = list(olds)
    for i in range(len(olds)):
        aliases[1 + len(operands) + i] = 1 + i
    if out is not None:
        aliases[1 + len(operands) + len(extra)] = 4
        extra.append(out)
    extra += list(unread)
    in_specs += [ANY] * (len(pieces) + len(extra))
    operands += extra
    return pl.pallas_call(
        functools.partial(
            step_kernel,
            inverse,
            units,
            slice_width,
            offset,
            unpack,
            n_acts,
            len(extra),
            [group[:2] for group in groups],
            n_steps,
        ),
        out_shape=tuple(out_shapes),
        grid_spec=pltpu.PrefetchScalarGridSpec(
            num_scalar_prefetch=1,
            grid=(n_steps,),
            in_specs=in_specs,
            out_specs=out_specs,
            scratch_shapes=place_scratch(groups),
        ),
        input_output_aliases=aliases,
        compiler_params=PARAMS,
        cost_estimate=pl.CostEstimate(
            flops=STEP_COST * width,
            bytes_accessed=rows * width * 30 + sum(piece.size for piece in pieces) * 4,
            transcendentals=rows * width,
        ),
        name="optimizer_step",
    )(ids, *operands)


def place_kernel(slice_width, layout, ids, *refs):
    n_pieces = sum(len(masks) for _, masks in layout)
    scratch = refs[n_pieces + 3 :]
    loads, stores = placements(
        ids, slice_width, layout, refs[:n_pieces], refs[n_pieces + 2], scratch
    )
    for load in loads:
        load.start()
    forward_copies(loads, stores)
    for store in stores:
        store.wait()


def place_pieces(ids, groups, slice_width, out, after):
    pieces = [piece for group in groups for piece in group[2]]
    size = sum(piece.size for piece in pieces)
    return pl.pallas_call(
        functools.partial(place_kernel, slice_width, [group[:2] for group in groups]),
        out_shape=jax.ShapeDtypeStruct(out.shape, out.dtype),
        grid_spec=pltpu.PrefetchScalarGridSpec(
            num_scalar_prefetch=1,
            grid=(),
            in_specs=[ANY] * (len(pieces) + 2),
            out_specs=ANY,
            scratch_shapes=place_scratch(groups),
        ),
        input_output_aliases={1 + len(pieces): 0},
        compiler_params=PARAMS,
        cost_estimate=pl.CostEstimate(
            flops=PLACE_COST * size, bytes_accessed=size * 4, transcendentals=0
        ),
        name="place_pieces",
    )(ids, *pieces, out, after)


def product_kernel(grads, weight, *rest):
    terms = rest[-1]
    product = jnp.dot(grads[...], weight[...], preferred_element_type=jnp.float32)
    terms[0] = product.astype(terms.dtype)


def input_product(grads, weight, slices, first, last, old, after):
    tokens, units = grads.shape
    width = weight.shape[1] // slices
    n_old = 0 if old is None else 1
    return pl.pallas_call(
        product_kernel,
        out_shape=jax.ShapeDtypeStruct((slices, tokens, width), jnp.bfloat16),
        grid=(last - first,),
        in_specs=[
            pl.BlockSpec((tokens, units), lambda j: (0, 0)),
            pl.BlockSpec((units, width), lambda j: (0, first + j)),
        ]
        + [ANY] * (n_old + 1),
        out_specs=pl.BlockSpec((1, tokens, width), lambda j: (first + j, 0, 0)),
        input_output_aliases={3: 0} if n_old else {},
        compiler_params=PARAMS,
        cost_estimate=pl.CostEstimate(
            flops=PRODUCT_COST * width * (last - first),
            bytes_accessed=units * width * (last - first) * 2,
            transcendentals=0,
        ),
        name="input_product",
    )(grads, weight, after, *([old] if n_old else []))


def square_body(activations, hidden_grad, weight, master, first_moment, second_moment, ema_state):
    batches, tok_rows, model_width = activations.shape
    shard_units = master.shape[0]
    n_dp = lax.axis_size("dp")
    n_tensor = lax.axis_size("tensor")
    n_pairs = n_tensor // 2
    tokens = batches * tok_rows
    inverse = 1.0 / (tokens * n_dp)
    width = model_width // n_tensor
    ids = jnp.stack([lax.axis_index("dp"), lax.axis_index("tensor")]).astype(jnp.int32)

    def swap(array, mask):
        return lax.ppermute(array, "dp", [(i, i ^ mask) for i in range(n_dp)])

    def swap_core(array):
        return lax.ppermute(array, "tensor", [(i, i ^ 1) for i in range(n_tensor)])

    def shift_pair(array, steps):
        moves = [(i, (i + 2 * steps) % n_tensor) for i in range(n_tensor)]
        return lax.ppermute(array, "tensor", moves)

    acts_two = activations.reshape(tokens, model_width)
    grads_two = hidden_grad.reshape(tokens, -1)
    messages = pack_messages(ids, acts_two, grads_two, n_dp, width)
    messages = [messages[0]] + [swap(messages[m], m) for m in range(1, n_dp)]
    acts, grads = None, None
    terms = input_product(grads_two, weight, n_tensor, 0, PRODUCT_FIRST, None, messages[0])

    states = (master, first_moment, second_moment, ema_state)
    shape = (n_dp, shard_units, model_width)
    olds, out, unread, sent, placed = (), None, (terms,), [], 0
    masks = tuple(range(n_dp))
    n_cuts = len(FIRST_CUTS) + len(LAST_CUTS) + n_tensor - 2
    for step in range(n_pairs):
        if step > 0:
            acts = shift_pair(acts, 1)
        for side in range(2):
            block = swap_core(acts) if side else acts
            chunk = 2 * step + side
            parts = FIRST_CUTS if chunk == 0 else LAST_CUTS if chunk == n_tensor - 1 else (4,)
            offset = 0
            for part in parts:
                cut = width * part // 4
                count = len(sent)
                where = (n_tensor, step, side, offset)
                until = max(count - LAG + 1, 0) + (LAST_MORE if count == n_cuts - 1 else 0)
                groups, placed = [(w, masks, p) for p, w in sent[placed:until]], max(until, placed)
                early = count < len(FIRST_CUTS)
                unpack = count == UNPACK_AT
                gate = tuple(sent[count - GATE][0][1:3]) if 0 < GATE <= count else ()
                results = optimizer_step(
                    inverse,
                    shard_units if early else None,
                    unpack,
                    ids,
                    where,
                    cut,
                    messages if early else [block],
                    grads,
                    states,
                    olds,
                    unread + gate,
                    groups,
                    shape,
                    out,
                )
                piece, olds = results[0], results[1:4]
                out = results[4] if groups else None
                if unpack:
                    acts, grads = results[-2:]
                unread = ()
                by_x, by_y = swap(piece, 1), swap(piece, 2)
                by_both = swap(by_y, 1) if FORWARD_BY_X[count] else swap(by_x, 2)
                sent.append(((piece, by_x, by_y, by_both), where))
                if count == PRODUCT_AT:
                    terms = input_product(
                        grads_two, weight, n_tensor, PRODUCT_FIRST, n_tensor, terms, piece
                    )
                    unread = (terms,)
                offset += cut
    terms = lax.all_to_all(terms, "tensor", 0, 0)
    d_inputs = jnp.sum(terms.astype(jnp.float32), axis=0).astype(jnp.bfloat16)
    groups = [(w, masks, p) for p, w in sent[placed:-1]]
    pieces, where = sent[-1]
    groups.append((where, masks[:3], pieces[:3]))
    if TAIL_SPLIT:
        out = place_pieces(ids, groups[:-TAIL_SPLIT], width, out, d_inputs)
        groups = groups[-TAIL_SPLIT:]
    out = place_pieces(ids, groups, width, out, d_inputs)
    out = place_pieces(ids, [(where, masks[3:], pieces[3:])], width, out, d_inputs)
    d_inputs = d_inputs.reshape(batches, tok_rows, width)
    ema_copy = out.reshape(n_dp * shard_units, model_width)

    return (d_inputs, *olds, ema_copy)


def general_body(activations, hidden_grad, weight, master, first_moment, second_moment, ema_state):
    batches, tok_rows, model_width = activations.shape
    shard_units = master.shape[0]
    inverse = 1.0 / (batches * tok_rows * lax.axis_size("dp"))
    pieces = []
    for batch_id in range(batches):
        product = jnp.dot(hidden_grad[batch_id], weight, preferred_element_type=jnp.float32)
        pieces.append(
            lax.psum_scatter(product, "tensor", scatter_dimension=1, tiled=True).astype(
                jnp.bfloat16
            )
        )
    d_inputs = jnp.stack(pieces)
    col_start = lax.axis_index("dp") * shard_units
    acts_piece = lax.all_gather(activations, "dp", axis=1, tiled=True)
    grad_piece = lax.all_gather(hidden_grad, "dp", axis=1, tiled=True)
    shards = acts_piece.shape[1] // tok_rows
    columns = lax.dynamic_slice_in_dim(grad_piece, col_start, shard_units, 2)
    acts_blocks = acts_piece.reshape(batches, shards, tok_rows, model_width)
    grad_blocks = columns.reshape(batches, shards, tok_rows, shard_units)
    per_shard = (
        jnp.einsum("bstf,bstd->sfd", grad_blocks, acts_blocks, preferred_element_type=jnp.float32)
        * inverse
    )
    rounded = lax.optimization_barrier(per_shard.astype(jnp.bfloat16))
    gradient = jnp.sum(rounded.astype(jnp.float32), axis=0)
    master_out, new_first, new_second, ema_next = adam(
        gradient, master, first_moment, second_moment, ema_state
    )
    ema_copy = lax.all_gather(ema_next.astype(jnp.bfloat16), "dp", axis=0, tiled=True)
    return (d_inputs, master_out, new_first, new_second, ema_copy)


def body(*arrays):
    activations, _, _, master = arrays[:4]
    n_tensor = lax.axis_size("tensor")
    square = (
        lax.axis_size("dp") == 4
        and n_tensor % 2 == 0
        and master.shape[0] % 8 == 0
        and activations.shape[2] % (n_tensor * 4 * LEAD) == 0
    )
    return square_body(*arrays) if square else general_body(*arrays)


def solution(mesh):
    return jax.shard_map(
        body,
        mesh=mesh,
        in_specs=(
            P(None, "dp", None),
            P(None, "dp", "tensor"),
            P("tensor", None),
            P(("tensor", "dp"), None),
            P(("tensor", "dp"), None),
            P(("tensor", "dp"), None),
            P(("tensor", "dp"), None),
        ),
        out_specs=(
            P(None, "dp", "tensor"),
            P(("tensor", "dp"), None),
            P(("tensor", "dp"), None),
            P(("tensor", "dp"), None),
            P("tensor", None),
        ),
        check_vma=False,
    )
```

```python
import functools

import jax
import jax.numpy as jnp
from jax import lax
from jax.experimental import pallas as pl
from jax.experimental.pallas import tpu as pltpu
from jax.sharding import PartitionSpec as P

beta_one = 0.9
beta_two = 0.95
adam_step = 20.0
learn_rate = 0.1
decay_rate = 0.1
epsilon = 1e-08
ema_keep = 0.99
first_fix = 1.0 - beta_one**adam_step
second_fix = 1.0 - beta_two**adam_step

LEAD = 256
LAG = 3
PRODUCT_FIRST = 6
PRODUCT_AT = 3
FIRST_CUTS = (2, 2)
LAST_CUTS = (4,)
UNPACK_AT = 0
GATE = 2
FORWARD_BY_X = (0, 1, 0, 1, 0, 1, 0, 1, 0, 1, 0, 1)
LAST_MORE = 0
TAIL = 2
GATE_MASKS = (2,)
Y_FIRST = 0
SPLIT_LAST = 0
STEP_COST = 8000000
PLACE_COST = 850
PRODUCT_COST = 6000000
VMEM_LIMIT = 63 * 1024 * 1024
ANY = pl.BlockSpec(memory_space=pl.ANY)
PARAMS = pltpu.CompilerParams(vmem_limit_bytes=VMEM_LIMIT)


def adam(gradient, master, first_moment, second_moment, ema_state):
    new_first = beta_one * first_moment + (1.0 - beta_one) * gradient
    new_second = beta_two * second_moment + (1.0 - beta_two) * gradient * gradient
    update = (
        new_first / first_fix / (jnp.sqrt(new_second / second_fix) + epsilon) + decay_rate * master
    )
    master_out = master - learn_rate * update
    ema_next = ema_keep * ema_state + (1.0 - ema_keep) * master_out
    return master_out, new_first, new_second, ema_next


def feature_of(ids, n_tensor, step, side):
    n_pairs = n_tensor // 2
    pair = lax.rem(lax.div(ids[1], 2) + (n_pairs - step), n_pairs)
    core = lax.rem(ids[1], 2)
    return 2 * pair + (1 - core if side else core)


def peer_of(dp, mask):
    high, low = lax.div(dp, 2), lax.rem(dp, 2)
    return 2 * (1 - high if mask & 2 else high) + (1 - low if mask & 1 else low)


def pack_kernel(units, width, ids, acts, grads, *messages):
    for mask, message in enumerate(messages):
        message[:, :width] = acts[...]
        for owner in range(len(messages)):

            @pl.when(peer_of(ids[0], mask) == owner)
            def _(owner=owner, message=message):
                message[:, width : width + units] = grads[:, owner * units : (owner + 1) * units]


def pack_messages(ids, acts, grads, n_dp, width):
    tokens, all_units = grads.shape
    units = all_units // n_dp
    message = jax.ShapeDtypeStruct((tokens, width + pl.cdiv(units, 128) * 128), acts.dtype)
    return pl.pallas_call(
        functools.partial(pack_kernel, units, width),
        out_shape=(message,) * n_dp,
        grid_spec=pltpu.PrefetchScalarGridSpec(
            num_scalar_prefetch=1,
            grid=(1,),
            in_specs=[
                pl.BlockSpec((tokens, width), lambda j, ids: (0, ids[1])),
                pl.BlockSpec((tokens, all_units), lambda j, ids: (0, 0)),
            ],
            out_specs=[pl.BlockSpec(message.shape, lambda j, ids: (0, 0))] * n_dp,
        ),
        compiler_params=PARAMS,
        cost_estimate=pl.CostEstimate(
            flops=0, bytes_accessed=tokens * all_units * 8, transcendentals=0
        ),
        name="pack_messages",
    )(ids, acts, grads)


def column_of(ids, where, slice_width):
    n_tensor, step, side, offset = where
    return pl.multiple_of(feature_of(ids, n_tensor, step, side) * slice_width + offset, LEAD)


def place_scratch(groups):
    scratch = []
    for _, masks, pieces in groups:
        scratch.append(pltpu.VMEM((len(masks),) + pieces[0].shape, pieces[0].dtype))
        scratch.append(pltpu.SemaphoreType.DMA((len(masks),)))
        scratch.append(pltpu.SemaphoreType.DMA((len(masks),)))
    return scratch


def placements(ids, slice_width, layout, pieces, out, scratch):
    loads, stores = [], []
    for i, (where, masks) in enumerate(layout):
        held, arrived, left = scratch[3 * i : 3 * i + 3]
        column = column_of(ids, where, slice_width)
        for j, mask in enumerate(masks):
            piece = pieces[len(loads)]
            goal = out.at[peer_of(ids[0], mask), :, pl.ds(column, piece.shape[1])]
            loads.append(pltpu.make_async_copy(piece, held.at[j], arrived.at[j]))
            stores.append(pltpu.make_async_copy(held.at[j], goal, left.at[j]))
    return loads, stores


def forward_copies(loads, stores):
    for load, store in zip(loads, stores):
        load.wait()
        store.start()


def step_kernel(
    inverse, units, slice_width, offset, unpack, n_acts, n_unread, layout, n_steps, ids, *refs
):
    acts = refs[:n_acts]
    refs = refs[n_acts:]
    if units is None:
        gradient = lambda: jnp.dot(refs[0][...], acts[0][...], preferred_element_type=jnp.float32)
        refs_states = refs[1:5]
        rest = refs[5:]
    else:

        def gradient():
            total = None
            for message in acts:
                term = lax.dot_general(
                    message[:, slice_width : slice_width + units],
                    message[:, offset : offset + tile],
                    (((0,), (0,)), ((), ())),
                    preferred_element_type=jnp.float32,
                )
                total = term if total is None else total + term
            return total

        refs_states = refs[:4]
        rest = refs[4:]
    master, first, second, ema = refs_states
    n_pieces = sum(len(masks) for _, masks in layout)
    pieces = rest[:n_pieces]
    rest = rest[n_pieces + n_unread :]
    piece, master_out, first_out, second_out = rest[:4]
    tile = piece.shape[1]
    step = pl.program_id(0)
    if n_pieces:
        loads, stores = placements(ids, slice_width, layout, pieces, rest[4], rest[5:])

        @pl.when(step == 0)
        def _():
            for load in loads:
                load.start()

        if n_steps > 1:

            @pl.when(step == n_steps - 1)
            def _():
                forward_copies(loads, stores)

    outs = adam(gradient() * inverse, master[...], first[...], second[...], ema[...])
    master_out[...] = outs[0]
    first_out[...] = outs[1]
    second_out[...] = outs[2]
    piece[...] = outs[3].astype(piece.dtype)
    if unpack:
        all_acts, all_grads = rest[-2:]
        tokens = acts[0].shape[0]
        for i, message in enumerate(acts):
            rows = slice(i * tokens, (i + 1) * tokens)
            all_acts[rows, :] = message[:, :slice_width]
            all_grads[:, rows] = message[:, slice_width : slice_width + units].T
    if n_pieces:

        @pl.when(step == n_steps - 1)
        def _():
            if n_steps == 1:
                forward_copies(loads, stores)
            for store in stores:
                store.wait()


def optimizer_step(
    inverse, units, unpack, ids, where, width, acts, grads, states, olds, unread, groups, whole_shape, out
):
    rows, model_width = states[0].shape
    n_tensor, step, side, offset = where
    slice_width = model_width // n_tensor
    tile = 2 * LEAD if width % (2 * LEAD) == 0 and offset % (2 * LEAD) == 0 else LEAD
    n_steps = width // tile

    def state_at(j, ids):
        return 0, feature_of(ids, n_tensor, step, side) * (slice_width // tile) + offset // tile + j

    def whole(array):
        return pl.BlockSpec(array.shape, lambda j, ids: (0,) * array.ndim)

    state_spec = pl.BlockSpec((rows, tile), state_at)
    if units is None:
        first_tile = offset // tile
        in_specs = [
            pl.BlockSpec((acts[0].shape[0], tile), lambda j, ids: (0, first_tile + j)),
            whole(grads),
        ]
        operands = [acts[0], grads]
    else:
        in_specs = [whole(message) for message in acts]
        operands = list(acts)
    n_acts = len(acts)
    operands += list(states)
    in_specs += [state_spec] * 4
    out_shapes = [jax.ShapeDtypeStruct((rows, width), jnp.bfloat16)]
    out_shapes += [jax.ShapeDtypeStruct((rows, model_width), jnp.float32)] * 3
    out_specs = [pl.BlockSpec((rows, tile), lambda j, ids: (0, j))] + [state_spec] * 3
    pieces = [piece for group in groups for piece in group[2]]
    if groups:
        out_shapes.append(jax.ShapeDtypeStruct(whole_shape, jnp.bfloat16))
        out_specs.append(ANY)
    if unpack:
        tokens = n_acts * acts[0].shape[0]
        for shape in ((tokens, slice_width), (units, tokens)):
            out_shapes.append(jax.ShapeDtypeStruct(shape, jnp.bfloat16))
            out_specs.append(pl.BlockSpec(shape, lambda j, ids: (0, 0)))
    operands += pieces
    aliases = {}
    extra = list(olds)
    for i in range(len(olds)):
        aliases[1 + len(operands) + i] = 1 + i
    if out is not None:
        aliases[1 + len(operands) + len(extra)] = 4
        extra.append(out)
    extra += list(unread)
    in_specs += [ANY] * (len(pieces) + len(extra))
    operands += extra
    return pl.pallas_call(
        functools.partial(
            step_kernel,
            inverse,
            units,
            slice_width,
            offset,
            unpack,
            n_acts,
            len(extra),
            [group[:2] for group in groups],
            n_steps,
        ),
        out_shape=tuple(out_shapes),
        grid_spec=pltpu.PrefetchScalarGridSpec(
            num_scalar_prefetch=1,
            grid=(n_steps,),
            in_specs=in_specs,
            out_specs=out_specs,
            scratch_shapes=place_scratch(groups),
        ),
        input_output_aliases=aliases,
        compiler_params=PARAMS,
        cost_estimate=pl.CostEstimate(
            flops=STEP_COST * width,
            bytes_accessed=rows * width * 30 + sum(piece.size for piece in pieces) * 4,
            transcendentals=rows * width,
        ),
        name="optimizer_step",
    )(ids, *operands)


def place_kernel(slice_width, layout, ids, *refs):
    n_pieces = sum(len(masks) for _, masks in layout)
    scratch = refs[n_pieces + 3 :]
    loads, stores = placements(
        ids, slice_width, layout, refs[:n_pieces], refs[n_pieces + 2], scratch
    )
    for load in loads:
        load.start()
    forward_copies(loads, stores)
    for store in stores:
        store.wait()


def place_pieces(ids, groups, slice_width, out, after):
    pieces = [piece for group in groups for piece in group[2]]
    size = sum(piece.size for piece in pieces)
    return pl.pallas_call(
        functools.partial(place_kernel, slice_width, [group[:2] for group in groups]),
        out_shape=jax.ShapeDtypeStruct(out.shape, out.dtype),
        grid_spec=pltpu.PrefetchScalarGridSpec(
            num_scalar_prefetch=1,
            grid=(),
            in_specs=[ANY] * (len(pieces) + 2),
            out_specs=ANY,
            scratch_shapes=place_scratch(groups),
        ),
        input_output_aliases={1 + len(pieces): 0},
        compiler_params=PARAMS,
        cost_estimate=pl.CostEstimate(
            flops=PLACE_COST * size, bytes_accessed=size * 4, transcendentals=0
        ),
        name="place_pieces",
    )(ids, *pieces, out, after)


def product_kernel(grads, weight, *rest):
    terms = rest[-1]
    product = jnp.dot(grads[...], weight[...], preferred_element_type=jnp.float32)
    terms[0] = product.astype(terms.dtype)


def input_product(grads, weight, slices, first, last, old, after):
    tokens, units = grads.shape
    width = weight.shape[1] // slices
    n_old = 0 if old is None else 1
    return pl.pallas_call(
        product_kernel,
        out_shape=jax.ShapeDtypeStruct((slices, tokens, width), jnp.bfloat16),
        grid=(last - first,),
        in_specs=[
            pl.BlockSpec((tokens, units), lambda j: (0, 0)),
            pl.BlockSpec((units, width), lambda j: (0, first + j)),
        ]
        + [ANY] * (n_old + 1),
        out_specs=pl.BlockSpec((1, tokens, width), lambda j: (first + j, 0, 0)),
        input_output_aliases={3: 0} if n_old else {},
        compiler_params=PARAMS,
        cost_estimate=pl.CostEstimate(
            flops=PRODUCT_COST * width * (last - first),
            bytes_accessed=units * width * (last - first) * 2,
            transcendentals=0,
        ),
        name="input_product",
    )(grads, weight, after, *([old] if n_old else []))


def square_body(activations, hidden_grad, weight, master, first_moment, second_moment, ema_state):
    batches, tok_rows, model_width = activations.shape
    shard_units = master.shape[0]
    n_dp = lax.axis_size("dp")
    n_tensor = lax.axis_size("tensor")
    n_pairs = n_tensor // 2
    tokens = batches * tok_rows
    inverse = 1.0 / (tokens * n_dp)
    width = model_width // n_tensor
    ids = jnp.stack([lax.axis_index("dp"), lax.axis_index("tensor")]).astype(jnp.int32)

    def swap(array, mask):
        return lax.ppermute(array, "dp", [(i, i ^ mask) for i in range(n_dp)])

    def swap_core(array):
        return lax.ppermute(array, "tensor", [(i, i ^ 1) for i in range(n_tensor)])

    def shift_pair(array, steps):
        moves = [(i, (i + 2 * steps) % n_tensor) for i in range(n_tensor)]
        return lax.ppermute(array, "tensor", moves)

    acts_two = activations.reshape(tokens, model_width)
    grads_two = hidden_grad.reshape(tokens, -1)
    messages = pack_messages(ids, acts_two, grads_two, n_dp, width)
    messages = [messages[0]] + [swap(messages[m], m) for m in range(1, n_dp)]
    acts, grads = None, None
    terms = input_product(grads_two, weight, n_tensor, 0, PRODUCT_FIRST, None, messages[0])

    states = (master, first_moment, second_moment, ema_state)
    shape = (n_dp, shard_units, model_width)
    olds, out, unread, sent, placed = (), None, (terms,), [], 0
    masks = tuple(range(n_dp))
    n_cuts = len(FIRST_CUTS) + len(LAST_CUTS) + n_tensor - 2
    for step in range(n_pairs):
        if step > 0:
            acts = shift_pair(acts, 1)
        for side in range(2):
            block = swap_core(acts) if side else acts
            chunk = 2 * step + side
            parts = FIRST_CUTS if chunk == 0 else LAST_CUTS if chunk == n_tensor - 1 else (4,)
            offset = 0
            for part in parts:
                cut = width * part // 4
                count = len(sent)
                where = (n_tensor, step, side, offset)
                until = max(count - LAG + 1, 0) + (LAST_MORE if count == n_cuts - 1 else 0)
                groups, placed = sum(sent[placed:until], []), max(until, placed)
                early = count < len(FIRST_CUTS)
                unpack = count == UNPACK_AT
                gate = ()
                if 0 < GATE <= count:
                    gate = tuple(sent[count - GATE][0][2][m] for m in GATE_MASKS)
                results = optimizer_step(
                    inverse,
                    shard_units if early else None,
                    unpack,
                    ids,
                    where,
                    cut,
                    messages if early else [block],
                    grads,
                    states,
                    olds,
                    unread + gate,
                    groups,
                    shape,
                    out,
                )
                piece, olds = results[0], results[1:4]
                out = results[4] if groups else None
                if unpack:
                    acts, grads = results[-2:]
                unread = ()
                if Y_FIRST:
                    by_y, by_x = swap(piece, 2), swap(piece, 1)
                else:
                    by_x, by_y = swap(piece, 1), swap(piece, 2)
                if count < n_cuts - SPLIT_LAST:
                    by_both = swap(by_y, 1) if FORWARD_BY_X[count] else swap(by_x, 2)
                    sent.append([(where, masks, (piece, by_x, by_y, by_both))])
                else:
                    half = cut // 2
                    middle = where[:3] + (offset + half,)
                    sent.append(
                        [
                            (where, masks[:3], (piece, by_x, by_y)),
                            (where, masks[3:], (swap(by_x[:, :half], 2),)),
                            (middle, masks[3:], (swap(by_y[:, half:], 1),)),
                        ]
                    )
                if count == PRODUCT_AT:
                    terms = input_product(
                        grads_two, weight, n_tensor, PRODUCT_FIRST, n_tensor, terms, piece
                    )
                    unread = (terms,)
                offset += cut
    terms = lax.all_to_all(terms, "tensor", 0, 0)
    d_inputs = jnp.sum(terms.astype(jnp.float32), axis=0).astype(jnp.bfloat16)
    if n_cuts - placed > TAIL:
        groups = sum(sent[placed : n_cuts - TAIL], [])
        out = place_pieces(ids, groups, width, out, d_inputs)
        placed = n_cuts - TAIL
    where, _, pieces = sent[-1][0]
    groups = sum(sent[placed:-1], []) + [(where, masks[:3], pieces[:3])]
    out = place_pieces(ids, groups, width, out, d_inputs)
    groups = sent[-1][1:] if SPLIT_LAST else [(where, masks[3:], pieces[3:])]
    out = place_pieces(ids, groups, width, out, d_inputs)
    d_inputs = d_inputs.reshape(batches, tok_rows, width)
    ema_copy = out.reshape(n_dp * shard_units, model_width)

    return (d_inputs, *olds, ema_copy)


def general_body(activations, hidden_grad, weight, master, first_moment, second_moment, ema_state):
    batches, tok_rows, model_width = activations.shape
    shard_units = master.shape[0]
    inverse = 1.0 / (batches * tok_rows * lax.axis_size("dp"))
    pieces = []
    for batch_id in range(batches):
        product = jnp.dot(hidden_grad[batch_id], weight, preferred_element_type=jnp.float32)
        pieces.append(
            lax.psum_scatter(product, "tensor", scatter_dimension=1, tiled=True).astype(
                jnp.bfloat16
            )
        )
    d_inputs = jnp.stack(pieces)
    col_start = lax.axis_index("dp") * shard_units
    acts_piece = lax.all_gather(activations, "dp", axis=1, tiled=True)
    grad_piece = lax.all_gather(hidden_grad, "dp", axis=1, tiled=True)
    shards = acts_piece.shape[1] // tok_rows
    columns = lax.dynamic_slice_in_dim(grad_piece, col_start, shard_units, 2)
    acts_blocks = acts_piece.reshape(batches, shards, tok_rows, model_width)
    grad_blocks = columns.reshape(batches, shards, tok_rows, shard_units)
    per_shard = (
        jnp.einsum("bstf,bstd->sfd", grad_blocks, acts_blocks, preferred_element_type=jnp.float32)
        * inverse
    )
    rounded = lax.optimization_barrier(per_shard.astype(jnp.bfloat16))
    gradient = jnp.sum(rounded.astype(jnp.float32), axis=0)
    master_out, new_first, new_second, ema_next = adam(
        gradient, master, first_moment, second_moment, ema_state
    )
    ema_copy = lax.all_gather(ema_next.astype(jnp.bfloat16), "dp", axis=0, tiled=True)
    return (d_inputs, master_out, new_first, new_second, ema_copy)


def body(*arrays):
    activations, _, _, master = arrays[:4]
    n_tensor = lax.axis_size("tensor")
    square = (
        lax.axis_size("dp") == 4
        and n_tensor % 2 == 0
        and master.shape[0] % 8 == 0
        and activations.shape[2] % (n_tensor * 4 * LEAD) == 0
    )
    return square_body(*arrays) if square else general_body(*arrays)


def solution(mesh):
    return jax.shard_map(
        body,
        mesh=mesh,
        in_specs=(
            P(None, "dp", None),
            P(None, "dp", "tensor"),
            P("tensor", None),
            P(("tensor", "dp"), None),
            P(("tensor", "dp"), None),
            P(("tensor", "dp"), None),
            P(("tensor", "dp"), None),
        ),
        out_specs=(
            P(None, "dp", "tensor"),
            P(("tensor", "dp"), None),
            P(("tensor", "dp"), None),
            P(("tensor", "dp"), None),
            P("tensor", None),
        ),
        check_vma=False,
    )
```

```python
import functools

import jax
import jax.numpy as jnp
from jax import lax
from jax.experimental import pallas as pl
from jax.experimental.pallas import tpu as pltpu
from jax.sharding import PartitionSpec as P

beta_one = 0.9
beta_two = 0.95
adam_step = 20.0
learn_rate = 0.1
decay_rate = 0.1
epsilon = 1e-08
ema_keep = 0.99
first_fix = 1.0 - beta_one**adam_step
second_fix = 1.0 - beta_two**adam_step

LEAD = 256
LAG = 3
PRODUCT_FIRST = 6
PRODUCT_AT = 3
FIRST_CUTS = (2, 2)
LAST_CUTS = (4,)
UNPACK_AT = 0
GATE = 2
FORWARD_BY_X = (0, 1, 0, 1, 0, 1, 0, 1, 0, 1, 0, 1)
LAST_MORE = 0
TAIL = 2
GATE_MASKS = (2,)
Y_FIRST = 0
SPLIT_LAST = 0
STEP_COST = 8000000
PLACE_COST = 850
PRODUCT_COST = 6000000
VMEM_LIMIT = 63 * 1024 * 1024
ANY = pl.BlockSpec(memory_space=pl.ANY)
PARAMS = pltpu.CompilerParams(vmem_limit_bytes=VMEM_LIMIT)


def adam(gradient, master, first_moment, second_moment, ema_state):
    new_first = beta_one * first_moment + (1.0 - beta_one) * gradient
    new_second = beta_two * second_moment + (1.0 - beta_two) * gradient * gradient
    update = (
        new_first / first_fix / (jnp.sqrt(new_second / second_fix) + epsilon) + decay_rate * master
    )
    master_out = master - learn_rate * update
    ema_next = ema_keep * ema_state + (1.0 - ema_keep) * master_out
    return master_out, new_first, new_second, ema_next


def feature_of(ids, n_tensor, step, side):
    n_pairs = n_tensor // 2
    pair = lax.rem(lax.div(ids[1], 2) + (n_pairs - step), n_pairs)
    core = lax.rem(ids[1], 2)
    return 2 * pair + (1 - core if side else core)


def peer_of(dp, mask):
    high, low = lax.div(dp, 2), lax.rem(dp, 2)
    return 2 * (1 - high if mask & 2 else high) + (1 - low if mask & 1 else low)


def pack_kernel(units, width, ids, acts, grads, *messages):
    for mask, message in enumerate(messages):
        message[:, :width] = acts[...]
        for owner in range(len(messages)):

            @pl.when(peer_of(ids[0], mask) == owner)
            def _(owner=owner, message=message):
                message[:, width : width + units] = grads[:, owner * units : (owner + 1) * units]


def pack_messages(ids, acts, grads, n_dp, width):
    tokens, all_units = grads.shape
    units = all_units // n_dp
    message = jax.ShapeDtypeStruct((tokens, width + pl.cdiv(units, 128) * 128), acts.dtype)
    return pl.pallas_call(
        functools.partial(pack_kernel, units, width),
        out_shape=(message,) * n_dp,
        grid_spec=pltpu.PrefetchScalarGridSpec(
            num_scalar_prefetch=1,
            grid=(1,),
            in_specs=[
                pl.BlockSpec((tokens, width), lambda j, ids: (0, ids[1])),
                pl.BlockSpec((tokens, all_units), lambda j, ids: (0, 0)),
            ],
            out_specs=[pl.BlockSpec(message.shape, lambda j, ids: (0, 0))] * n_dp,
        ),
        compiler_params=PARAMS,
        cost_estimate=pl.CostEstimate(
            flops=0, bytes_accessed=tokens * all_units * 8, transcendentals=0
        ),
        name="pack_messages",
    )(ids, acts, grads)


def column_of(ids, where, slice_width):
    n_tensor, step, side, offset = where
    return pl.multiple_of(feature_of(ids, n_tensor, step, side) * slice_width + offset, LEAD)


def place_scratch(groups):
    scratch = []
    for _, masks, pieces in groups:
        scratch.append(pltpu.VMEM((len(masks),) + pieces[0].shape, pieces[0].dtype))
        scratch.append(pltpu.SemaphoreType.DMA((len(masks),)))
        scratch.append(pltpu.SemaphoreType.DMA((len(masks),)))
    return scratch


def placements(ids, slice_width, layout, pieces, out, scratch):
    loads, stores = [], []
    for i, (where, masks) in enumerate(layout):
        held, arrived, left = scratch[3 * i : 3 * i + 3]
        column = column_of(ids, where, slice_width)
        for j, mask in enumerate(masks):
            piece = pieces[len(loads)]
            goal = out.at[peer_of(ids[0], mask), :, pl.ds(column, piece.shape[1])]
            loads.append(pltpu.make_async_copy(piece, held.at[j], arrived.at[j]))
            stores.append(pltpu.make_async_copy(held.at[j], goal, left.at[j]))
    return loads, stores


def forward_copies(loads, stores):
    for load, store in zip(loads, stores):
        load.wait()
        store.start()


def step_kernel(
    inverse, units, slice_width, offset, unpack, n_acts, n_unread, layout, n_steps, ids, *refs
):
    acts = refs[:n_acts]
    refs = refs[n_acts:]
    if units is None:
        gradient = lambda: jnp.dot(refs[0][...], acts[0][...], preferred_element_type=jnp.float32)
        refs_states = refs[1:5]
        rest = refs[5:]
    else:

        def gradient():
            total = None
            for message in acts:
                term = lax.dot_general(
                    message[:, slice_width : slice_width + units],
                    message[:, pl.ds(pl.multiple_of(offset + step * tile, tile), tile)],
                    (((0,), (0,)), ((), ())),
                    preferred_element_type=jnp.float32,
                )
                total = term if total is None else total + term
            return total

        refs_states = refs[:4]
        rest = refs[4:]
    master, first, second, ema = refs_states
    n_pieces = sum(len(masks) for _, masks in layout)
    pieces = rest[:n_pieces]
    rest = rest[n_pieces + n_unread :]
    piece, master_out, first_out, second_out = rest[:4]
    tile = piece.shape[1]
    step = pl.program_id(0)
    if n_pieces:
        loads, stores = placements(ids, slice_width, layout, pieces, rest[4], rest[5:])

        @pl.when(step == 0)
        def _():
            for load in loads:
                load.start()

        if n_steps > 1:

            @pl.when(step == n_steps - 1)
            def _():
                forward_copies(loads, stores)

    outs = adam(gradient() * inverse, master[...], first[...], second[...], ema[...])
    master_out[...] = outs[0]
    first_out[...] = outs[1]
    second_out[...] = outs[2]
    piece[...] = outs[3].astype(piece.dtype)
    if unpack:

        @pl.when(step == 0)
        def _():
            all_acts, all_grads = rest[-2:]
            tokens = acts[0].shape[0]
            for i, message in enumerate(acts):
                rows = slice(i * tokens, (i + 1) * tokens)
                all_acts[rows, :] = message[:, :slice_width]
                all_grads[:, rows] = message[:, slice_width : slice_width + units].T

    if n_pieces:

        @pl.when(step == n_steps - 1)
        def _():
            if n_steps == 1:
                forward_copies(loads, stores)
            for store in stores:
                store.wait()


def optimizer_step(
    inverse, units, unpack, ids, where, width, acts, grads, states, olds, unread, groups, whole_shape, out
):
    rows, model_width = states[0].shape
    n_tensor, step, side, offset = where
    slice_width = model_width // n_tensor
    wide = units is None and width % (2 * LEAD) == 0 and offset % (2 * LEAD) == 0
    tile = 2 * LEAD if wide else LEAD
    n_steps = width // tile

    def state_at(j, ids):
        return 0, feature_of(ids, n_tensor, step, side) * (slice_width // tile) + offset // tile + j

    def whole(array):
        return pl.BlockSpec(array.shape, lambda j, ids: (0,) * array.ndim)

    state_spec = pl.BlockSpec((rows, tile), state_at)
    if units is None:
        first_tile = offset // tile
        in_specs = [
            pl.BlockSpec((acts[0].shape[0], tile), lambda j, ids: (0, first_tile + j)),
            whole(grads),
        ]
        operands = [acts[0], grads]
    else:
        in_specs = [whole(message) for message in acts]
        operands = list(acts)
    n_acts = len(acts)
    operands += list(states)
    in_specs += [state_spec] * 4
    out_shapes = [jax.ShapeDtypeStruct((rows, width), jnp.bfloat16)]
    out_shapes += [jax.ShapeDtypeStruct((rows, model_width), jnp.float32)] * 3
    out_specs = [pl.BlockSpec((rows, tile), lambda j, ids: (0, j))] + [state_spec] * 3
    pieces = [piece for group in groups for piece in group[2]]
    if groups:
        out_shapes.append(jax.ShapeDtypeStruct(whole_shape, jnp.bfloat16))
        out_specs.append(ANY)
    if unpack:
        tokens = n_acts * acts[0].shape[0]
        for shape in ((tokens, slice_width), (units, tokens)):
            out_shapes.append(jax.ShapeDtypeStruct(shape, jnp.bfloat16))
            out_specs.append(pl.BlockSpec(shape, lambda j, ids: (0, 0)))
    operands += pieces
    aliases = {}
    extra = list(olds)
    for i in range(len(olds)):
        aliases[1 + len(operands) + i] = 1 + i
    if out is not None:
        aliases[1 + len(operands) + len(extra)] = 4
        extra.append(out)
    extra += list(unread)
    in_specs += [ANY] * (len(pieces) + len(extra))
    operands += extra
    return pl.pallas_call(
        functools.partial(
            step_kernel,
            inverse,
            units,
            slice_width,
            offset,
            unpack,
            n_acts,
            len(extra),
            [group[:2] for group in groups],
            n_steps,
        ),
        out_shape=tuple(out_shapes),
        grid_spec=pltpu.PrefetchScalarGridSpec(
            num_scalar_prefetch=1,
            grid=(n_steps,),
            in_specs=in_specs,
            out_specs=out_specs,
            scratch_shapes=place_scratch(groups),
        ),
        input_output_aliases=aliases,
        compiler_params=PARAMS,
        cost_estimate=pl.CostEstimate(
            flops=STEP_COST * width,
            bytes_accessed=rows * width * 30 + sum(piece.size for piece in pieces) * 4,
            transcendentals=rows * width,
        ),
        name="optimizer_step",
    )(ids, *operands)


def place_kernel(slice_width, layout, ids, *refs):
    n_pieces = sum(len(masks) for _, masks in layout)
    scratch = refs[n_pieces + 3 :]
    loads, stores = placements(
        ids, slice_width, layout, refs[:n_pieces], refs[n_pieces + 2], scratch
    )
    for load in loads:
        load.start()
    forward_copies(loads, stores)
    for store in stores:
        store.wait()


def place_pieces(ids, groups, slice_width, out, after):
    pieces = [piece for group in groups for piece in group[2]]
    size = sum(piece.size for piece in pieces)
    return pl.pallas_call(
        functools.partial(place_kernel, slice_width, [group[:2] for group in groups]),
        out_shape=jax.ShapeDtypeStruct(out.shape, out.dtype),
        grid_spec=pltpu.PrefetchScalarGridSpec(
            num_scalar_prefetch=1,
            grid=(),
            in_specs=[ANY] * (len(pieces) + 2),
            out_specs=ANY,
            scratch_shapes=place_scratch(groups),
        ),
        input_output_aliases={1 + len(pieces): 0},
        compiler_params=PARAMS,
        cost_estimate=pl.CostEstimate(
            flops=PLACE_COST * size, bytes_accessed=size * 4, transcendentals=0
        ),
        name="place_pieces",
    )(ids, *pieces, out, after)


def product_kernel(grads, weight, *rest):
    terms = rest[-1]
    product = jnp.dot(grads[...], weight[...], preferred_element_type=jnp.float32)
    terms[0] = product.astype(terms.dtype)


def input_product(grads, weight, slices, first, last, old, after):
    tokens, units = grads.shape
    width = weight.shape[1] // slices
    n_old = 0 if old is None else 1
    return pl.pallas_call(
        product_kernel,
        out_shape=jax.ShapeDtypeStruct((slices, tokens, width), jnp.bfloat16),
        grid=(last - first,),
        in_specs=[
            pl.BlockSpec((tokens, units), lambda j: (0, 0)),
            pl.BlockSpec((units, width), lambda j: (0, first + j)),
        ]
        + [ANY] * (n_old + 1),
        out_specs=pl.BlockSpec((1, tokens, width), lambda j: (first + j, 0, 0)),
        input_output_aliases={3: 0} if n_old else {},
        compiler_params=PARAMS,
        cost_estimate=pl.CostEstimate(
            flops=PRODUCT_COST * width * (last - first),
            bytes_accessed=units * width * (last - first) * 2,
            transcendentals=0,
        ),
        name="input_product",
    )(grads, weight, after, *([old] if n_old else []))


def square_body(activations, hidden_grad, weight, master, first_moment, second_moment, ema_state):
    batches, tok_rows, model_width = activations.shape
    shard_units = master.shape[0]
    n_dp = lax.axis_size("dp")
    n_tensor = lax.axis_size("tensor")
    n_pairs = n_tensor // 2
    tokens = batches * tok_rows
    inverse = 1.0 / (tokens * n_dp)
    width = model_width // n_tensor
    ids = jnp.stack([lax.axis_index("dp"), lax.axis_index("tensor")]).astype(jnp.int32)

    def swap(array, mask):
        return lax.ppermute(array, "dp", [(i, i ^ mask) for i in range(n_dp)])

    def swap_core(array):
        return lax.ppermute(array, "tensor", [(i, i ^ 1) for i in range(n_tensor)])

    def shift_pair(array, steps):
        moves = [(i, (i + 2 * steps) % n_tensor) for i in range(n_tensor)]
        return lax.ppermute(array, "tensor", moves)

    acts_two = activations.reshape(tokens, model_width)
    grads_two = hidden_grad.reshape(tokens, -1)
    messages = pack_messages(ids, acts_two, grads_two, n_dp, width)
    messages = [messages[0]] + [swap(messages[m], m) for m in range(1, n_dp)]
    acts, grads = None, None
    terms = input_product(grads_two, weight, n_tensor, 0, PRODUCT_FIRST, None, messages[0])

    states = (master, first_moment, second_moment, ema_state)
    shape = (n_dp, shard_units, model_width)
    olds, out, unread, sent, placed = (), None, (terms,), [], 0
    masks = tuple(range(n_dp))
    n_cuts = len(FIRST_CUTS) + len(LAST_CUTS) + n_tensor - 2
    for step in range(n_pairs):
        if step > 0:
            acts = shift_pair(acts, 1)
        for side in range(2):
            block = swap_core(acts) if side else acts
            chunk = 2 * step + side
            parts = FIRST_CUTS if chunk == 0 else LAST_CUTS if chunk == n_tensor - 1 else (4,)
            offset = 0
            for part in parts:
                cut = width * part // 4
                count = len(sent)
                where = (n_tensor, step, side, offset)
                until = max(count - LAG + 1, 0) + (LAST_MORE if count == n_cuts - 1 else 0)
                groups, placed = sum(sent[placed:until], []), max(until, placed)
                early = count < len(FIRST_CUTS)
                unpack = count == UNPACK_AT
                gate = ()
                if 0 < GATE <= count:
                    gate = tuple(sent[count - GATE][0][2][m] for m in GATE_MASKS)
                results = optimizer_step(
                    inverse,
                    shard_units if early else None,
                    unpack,
                    ids,
                    where,
                    cut,
                    messages if early else [block],
                    grads,
                    states,
                    olds,
                    unread + gate,
                    groups,
                    shape,
                    out,
                )
                piece, olds = results[0], results[1:4]
                out = results[4] if groups else None
                if unpack:
                    acts, grads = results[-2:]
                unread = ()
                if Y_FIRST:
                    by_y, by_x = swap(piece, 2), swap(piece, 1)
                else:
                    by_x, by_y = swap(piece, 1), swap(piece, 2)
                if count < n_cuts - SPLIT_LAST:
                    by_both = swap(by_y, 1) if FORWARD_BY_X[count] else swap(by_x, 2)
                    sent.append([(where, masks, (piece, by_x, by_y, by_both))])
                else:
                    half = cut // 2
                    middle = where[:3] + (offset + half,)
                    sent.append(
                        [
                            (where, masks[:3], (piece, by_x, by_y)),
                            (where, masks[3:], (swap(by_x[:, :half], 2),)),
                            (middle, masks[3:], (swap(by_y[:, half:], 1),)),
                        ]
                    )
                if count == PRODUCT_AT:
                    terms = input_product(
                        grads_two, weight, n_tensor, PRODUCT_FIRST, n_tensor, terms, piece
                    )
                    unread = (terms,)
                offset += cut
    terms = lax.all_to_all(terms, "tensor", 0, 0)
    d_inputs = jnp.sum(terms.astype(jnp.float32), axis=0).astype(jnp.bfloat16)
    if n_cuts - placed > TAIL:
        groups = sum(sent[placed : n_cuts - TAIL], [])
        out = place_pieces(ids, groups, width, out, d_inputs)
        placed = n_cuts - TAIL
    where, _, pieces = sent[-1][0]
    groups = sum(sent[placed:-1], []) + [(where, masks[:3], pieces[:3])]
    out = place_pieces(ids, groups, width, out, d_inputs)
    groups = sent[-1][1:] if SPLIT_LAST else [(where, masks[3:], pieces[3:])]
    out = place_pieces(ids, groups, width, out, d_inputs)
    d_inputs = d_inputs.reshape(batches, tok_rows, width)
    ema_copy = out.reshape(n_dp * shard_units, model_width)

    return (d_inputs, *olds, ema_copy)


def general_body(activations, hidden_grad, weight, master, first_moment, second_moment, ema_state):
    batches, tok_rows, model_width = activations.shape
    shard_units = master.shape[0]
    inverse = 1.0 / (batches * tok_rows * lax.axis_size("dp"))
    pieces = []
    for batch_id in range(batches):
        product = jnp.dot(hidden_grad[batch_id], weight, preferred_element_type=jnp.float32)
        pieces.append(
            lax.psum_scatter(product, "tensor", scatter_dimension=1, tiled=True).astype(
                jnp.bfloat16
            )
        )
    d_inputs = jnp.stack(pieces)
    col_start = lax.axis_index("dp") * shard_units
    acts_piece = lax.all_gather(activations, "dp", axis=1, tiled=True)
    grad_piece = lax.all_gather(hidden_grad, "dp", axis=1, tiled=True)
    shards = acts_piece.shape[1] // tok_rows
    columns = lax.dynamic_slice_in_dim(grad_piece, col_start, shard_units, 2)
    acts_blocks = acts_piece.reshape(batches, shards, tok_rows, model_width)
    grad_blocks = columns.reshape(batches, shards, tok_rows, shard_units)
    per_shard = (
        jnp.einsum("bstf,bstd->sfd", grad_blocks, acts_blocks, preferred_element_type=jnp.float32)
        * inverse
    )
    rounded = lax.optimization_barrier(per_shard.astype(jnp.bfloat16))
    gradient = jnp.sum(rounded.astype(jnp.float32), axis=0)
    master_out, new_first, new_second, ema_next = adam(
        gradient, master, first_moment, second_moment, ema_state
    )
    ema_copy = lax.all_gather(ema_next.astype(jnp.bfloat16), "dp", axis=0, tiled=True)
    return (d_inputs, master_out, new_first, new_second, ema_copy)


def body(*arrays):
    activations, _, _, master = arrays[:4]
    n_tensor = lax.axis_size("tensor")
    square = (
        lax.axis_size("dp") == 4
        and n_tensor % 2 == 0
        and master.shape[0] % 8 == 0
        and activations.shape[2] % (n_tensor * 4 * LEAD) == 0
    )
    return square_body(*arrays) if square else general_body(*arrays)


def solution(mesh):
    return jax.shard_map(
        body,
        mesh=mesh,
        in_specs=(
            P(None, "dp", None),
            P(None, "dp", "tensor"),
            P("tensor", None),
            P(("tensor", "dp"), None),
            P(("tensor", "dp"), None),
            P(("tensor", "dp"), None),
            P(("tensor", "dp"), None),
        ),
        out_specs=(
            P(None, "dp", "tensor"),
            P(("tensor", "dp"), None),
            P(("tensor", "dp"), None),
            P(("tensor", "dp"), None),
            P("tensor", None),
        ),
        check_vma=False,
    )
```
